32 devices in a mesh: sec: 16 (over z, x, core), mpo: 2 (over y).
Axes of the slice: x: 2, y: 2, z: 4, core: 2. Of those that a mesh axis runs over, the one named last changes fastest.
Arguments:
- wavefunction: bfloat16 [1280, 128, 128], P('sec'), may hold values from -6 to 6
- left_sector: int32 [1280], P('sec'), may hold values from 0 to 159, as said below
- right_sector: int32 [1280], P('sec'), may hold values from 0 to 159, as said below
- term_mask: int32 [4, 160], P('mpo', 'sec'), may hold values 0 or 1
- left_operators: bfloat16 [4, 160, 128, 128], P('mpo', 'sec'), may hold values from -0.5 to 0.5
- right_operators: bfloat16 [4, 160, 128, 128], P('mpo', 'sec'), may hold values from -0.375 to 0.375
Outputs:
- applied: bfloat16 [1280, 128, 128], P('sec', 'mpo')
The draws below stay inside these ranges and needn't reach their ends.
Inputs may be any that keep to these rules, and one draw needn't show every extreme that they name: `left_sector`: the blocks 80 * d to 80 * d + 79 have left sectors from 10 * d to 10 * d + 9. `right_sector`: among the blocks 80 * d to 80 * d + 79, at most 10 have right sectors in any one range 10 * e to 10 * e + 9; for one e, drawn from the seed, every d has exactly 10 there.
All inputs are finite; a program needn't handle non-finite values. No bound on the sum of `term_mask` on one device may be relied on, other than what follows from the above.
Results may differ from the reference program's by a relative error of at most 0.015.
Values may be sent and summed in bfloat16 or wider, within the bound.
No kernel may reach another device: no remote copies, remote signals or barrier semaphores. Data moves between devices by JAX's collectives and lax.ppermute only.
A program may use at most 128 MiB of HBM per device.

```python
import jax
import jax.numpy as jnp
from jax import lax

SB = 128
TERM_DEV = 2
BLK_DEV = 80
SEC_DEV = 10
NLS = 160
NBLK = 1280
TERMS = 4


def sector_pairs(key):
    owners_total = NLS // SEC_DEV
    full_owner = jax.random.randint(jax.random.fold_in(key, 11), (), 0, owners_total)

    def for_device(device):
        device_key = jax.random.fold_in(key, device + 1000)
        others = jax.random.permutation(jax.random.fold_in(device_key, 1), NLS - SEC_DEV).astype(jnp.int32)
        others = others + SEC_DEV * (others >= full_owner * SEC_DEV).astype(jnp.int32)
        forced = full_owner * SEC_DEV + jnp.arange(SEC_DEV, dtype=jnp.int32)
        chosen = jnp.concatenate([forced, others[:BLK_DEV - SEC_DEV]])
        ordering = jax.random.permutation(jax.random.fold_in(device_key, 2), BLK_DEV)
        chosen = chosen[ordering]
        target = chosen // SEC_DEV
        rights = target * SEC_DEV + jax.random.randint(jax.random.fold_in(device_key, 3), (BLK_DEV,), 0, SEC_DEV)
        left_ids = device * SEC_DEV + jax.random.randint(jax.random.fold_in(device_key, 4), (BLK_DEV,), 0, SEC_DEV)
        return (left_ids.astype(jnp.int32), rights.astype(jnp.int32))
    left_ids, rights = jax.vmap(for_device)(jnp.arange(owners_total, dtype=jnp.int32))
    return (left_ids.reshape(-1), rights.reshape(-1))


def draw_left_sector(key, part):
    return sector_pairs(key)[0]


def draw_right_sector(key, part):
    return sector_pairs(key)[1]


def set_ends(values, own_key, smallest, top_value):
    index_at = [jax.random.randint(jax.random.fold_in(own_key, axis), (), 0, length) for axis, length in enumerate(values.shape)]
    longest = values.shape.index(max(values.shape))
    neighbour = index_at[:longest] + [(index_at[longest] + 1) % values.shape[longest]] + index_at[longest + 1:]
    return values.at[tuple(index_at)].set(smallest).at[tuple(neighbour)].set(top_value)


def level_of(rng, dims, cuts, smallest, top_value):
    def one(dim, parts):
        draws = jax.random.uniform(jax.random.fold_in(jax.random.fold_in(rng, 6), dim), (parts,), jnp.float32, smallest / len(cuts), top_value / len(cuts))
        return jnp.repeat(jnp.exp(draws), dims[dim] // parts).reshape((-1,) + (1,) * (len(dims) - dim - 1))

    loudness = one(*cuts[0])
    for cut in cuts[1:]:
        loudness = loudness * one(*cut)
    return loudness


def noise(own_key, dims, width, limit, cuts=(), kind=jnp.bfloat16):
    drawn = width * jax.random.normal(own_key, dims, jnp.float32)
    if cuts:
        drawn = drawn * level_of(own_key, dims, cuts, -0.22, 0.18)
    return jnp.clip(drawn, -limit, limit).astype(kind)


def setup_inputs(seed: int = 0) -> dict:
    splits = jax.random.split(jax.random.key(seed), 7)
    wavefunction = noise(splits[0], (NBLK, SB, SB), 1.0, 6.0, ((0, 16),))
    left_sector = draw_left_sector(jax.random.fold_in(splits[6], 71), 0)
    right_sector = draw_right_sector(jax.random.fold_in(splits[6], 71), 0)
    term_mask = set_ends((jax.random.randint(splits[3], (TERMS, NLS), 0, 2) < 1).astype(jnp.int32), jax.random.fold_in(splits[3], 1), 0, 1)
    left_operators = noise(splits[4], (TERMS, NLS, SB, SB), SB ** -0.5, 0.5, ((0, 2), (1, 16)))
    right_operators = noise(splits[5], (TERMS, NLS, SB, SB), (SB * TERMS // 2) ** -0.5, 0.375, ((0, 2), (1, 16)))
    return dict(wavefunction=wavefunction, left_sector=left_sector, right_sector=right_sector, term_mask=term_mask, left_operators=left_operators, right_operators=right_operators)


def reference(wavefunction, left_sector, right_sector, term_mask, left_operators, right_operators):
    group_count = TERMS // TERM_DEV

    def one_group(inputs):
        blocks, left_ids, right_ids = inputs
        chosen_left = jnp.take(left_operators, left_ids, axis=1).astype(jnp.float32)
        weights = jnp.take(term_mask, left_ids, axis=1).astype(jnp.float32)
        left_full = jnp.einsum("kbij,bjc->kbic", chosen_left, blocks.astype(jnp.float32))
        left_part = (left_full * weights[:, :, None, None]).astype(jnp.bfloat16)
        left_part = lax.optimization_barrier(left_part).astype(jnp.float32)
        chosen_right = jnp.take(right_operators, right_ids, axis=1).astype(jnp.float32)
        right_part = jnp.einsum("kbij,kbcj->kbic", left_part, chosen_right)
        group_part = jnp.sum(right_part.reshape((group_count, TERM_DEV) + right_part.shape[1:]), axis=1)
        group_part = lax.optimization_barrier(group_part.astype(jnp.bfloat16)).astype(jnp.float32)
        return jnp.sum(group_part, axis=0).astype(jnp.bfloat16)

    shaped = wavefunction.reshape(-1, BLK_DEV, SB, SB)
    lefts_shaped = left_sector.reshape(-1, BLK_DEV).astype(jnp.int32)
    rights_shaped = right_sector.reshape(-1, BLK_DEV).astype(jnp.int32)
    result = lax.map(one_group, (shaped, lefts_shaped, rights_shaped))
    return result.reshape(NBLK, SB, SB)
```

```python
import functools

import jax
import jax.numpy as jnp
import numpy as np
from jax import lax
from jax.experimental import pallas as pl
from jax.experimental.pallas import tpu as pltpu
from jax.sharding import PartitionSpec as P

WIDTHS = (64, 64)
RING_LIMIT = 16
VMEM_LIMIT = 48 * 1024 * 1024


def chip_ring(chips):
    across = 2 if chips % 2 == 0 else 1
    up = [z * across for z in range(chips // across)]
    down = [z * across + 1 for z in reversed(range(chips // across))] if across == 2 else []
    return up + down


def ring_gather(part, forward_steps, chips):
    order = chip_ring(chips)
    after = {order[i]: order[(i + 1) % chips] for i in range(chips)}
    before = {order[i]: order[i - 1] for i in range(chips)}
    devices = range(2 * chips)
    forward = [(d, 2 * after[d // 2] + d % 2) for d in devices]
    backward = [(d, 2 * before[d // 2] + d % 2) for d in devices]
    swap = [(d, d ^ 1) for d in devices]
    ahead, behind, pieces, shifts = part, part, [part], [0]
    for step in range(1, chips):
        if step <= forward_steps:
            ahead = lax.ppermute(ahead, "sec", forward)
            pieces.append(ahead)
            shifts.append(-step)
        if step < chips - forward_steps:
            behind = lax.ppermute(behind, "sec", backward)
            pieces.append(behind)
            shifts.append(step)
    pieces = pieces + [lax.ppermute(piece, "sec", swap) for piece in pieces]
    place = {chip: i for i, chip in enumerate(order)}
    owners = np.zeros((2 * chips, len(pieces)), np.int32)
    for d in devices:
        for number, shift in enumerate(shifts):
            chip = order[(place[d // 2] + shift) % chips]
            owners[d, number] = 2 * chip + d % 2
            owners[d, number + len(shifts)] = 2 * chip + 1 - d % 2
    return pieces, owners


def left_kernel(here_ref, sector_ref, mask_ref, operator_ref, wave_ref, out_ref, *, parties):
    terms, sectors, width, _ = operator_ref.shape
    blocks = wave_ref.shape[0]
    rows = width // parties
    own, first = here_ref[0], here_ref[1] * sectors

    def one_block(b, carry):
        local = sector_ref[b] - first
        bands = [
            operator_ref[k, local, pl.ds(pl.multiple_of(lax.rem(own + j, parties) * rows, rows), rows), :]
            for k in range(terms)
            for j in range(parties)
        ]
        product = jnp.dot(
            jnp.concatenate(bands, axis=0), wave_ref[b], preferred_element_type=jnp.float32
        )
        for k in range(terms):
            weight = mask_ref[k, local].astype(jnp.float32)
            out_ref[b, :, k * width : (k + 1) * width] = (
                product[k * width : (k + 1) * width] * weight
            ).astype(out_ref.dtype)
        return carry

    lax.fori_loop(0, blocks, one_block, 0, unroll=8)


def right_kernel(owner_ref, sector_ref, left_ref, *refs, pieces, parties):
    piece_refs, out_refs = refs[:pieces], refs[pieces : pieces + parties]
    held, arrived = refs[pieces + parties :]
    terms, _, columns, width = held.shape
    sectors = piece_refs[0].shape[1]
    blocks, rows = left_ref.shape[0], left_ref.shape[1] // parties
    pack = width // columns
    copies = [
        pltpu.make_async_copy(
            piece, held.at[:, pl.ds(owner_ref[number] * sectors, sectors)], arrived.at[number]
        )
        for number, piece in enumerate(piece_refs)
    ]
    for copy in copies:
        copy.start()
    for copy in copies:
        copy.wait()
    lane = lax.broadcasted_iota(jnp.int32, (left_ref.shape[1], width), 1) // columns

    def one_group(g, carry):
        factors = []
        for q in range(pack):
            sector = sector_ref[g * pack + q]
            factors.append(jnp.concatenate([held[k, sector] for k in range(terms)], axis=1))
        factor = jnp.concatenate(factors, axis=0)
        lefts = jnp.concatenate([left_ref[g * pack + q] for q in range(pack)], axis=0)
        product = lax.dot_general(
            lefts, factor, (((1,), (1,)), ((), ())), preferred_element_type=jnp.float32
        ).reshape(pack, left_ref.shape[1], width)
        chosen = product[0]
        for q in range(1, pack):
            chosen = jnp.where(lane == q, product[q], chosen)
        for j in range(parties):
            out_refs[j][g] = chosen[j * rows : (j + 1) * rows].astype(out_refs[j].dtype)
        return carry

    lax.fori_loop(0, blocks // pack, one_group, 0, unroll=4)


def join_kernel(*refs, widths, parties):
    out_ref = refs[-1]
    blocks, rows, width = out_ref.shape
    parts = [refs[c * parties : (c + 1) * parties] for c in range(len(widths))]
    most = max(width // columns for columns in widths)
    lane = lax.broadcasted_iota(jnp.int32, (rows, width), 1)

    def one_group(g, carry):
        sums = []
        for columns, given in zip(widths, parts):
            pack = width // columns
            inside = []
            for t in range(most // pack):
                total = given[0][g * (most // pack) + t].astype(jnp.float32)
                for other in given[1:]:
                    total = total + other[g * (most // pack) + t].astype(jnp.float32)
                inside.append(total)
            sums.append(inside)
        for b in range(most):
            start, value = 0, None
            for columns, inside in zip(widths, sums):
                pack = width // columns
                source, q = inside[b // pack], b % pack
                turn = (start - q * columns) % width
                moved = pltpu.roll(source, turn, 1) if turn else source
                value = moved if value is None else jnp.where(lane >= start, moved, value)
                start += columns
            out_ref[g * most + b] = value.astype(out_ref.dtype)
        return carry

    lax.fori_loop(0, blocks // most, one_group, 0, unroll=4)


def on_device(wavefunction, left_sector, right_sector, term_mask, left_operators, right_operators):
    owners, parties = lax.axis_size("sec"), lax.axis_size("mpo")
    me, own = lax.axis_index("sec"), lax.axis_index("mpo")
    terms, sectors, width, _ = left_operators.shape
    blocks = wavefunction.shape[0]
    rows = width // parties
    smem = pl.BlockSpec(memory_space=pltpu.SMEM)
    vmem = pl.BlockSpec(memory_space=pltpu.VMEM)
    anywhere = pl.BlockSpec(memory_space=pl.ANY)
    params = pltpu.CompilerParams(vmem_limit_bytes=VMEM_LIMIT)

    left_part = pl.pallas_call(
        functools.partial(left_kernel, parties=parties),
        out_shape=jax.ShapeDtypeStruct((blocks, width, terms * width), jnp.bfloat16),
        in_specs=[smem, smem, smem, vmem, vmem],
        out_specs=vmem,
        compiler_params=params,
        cost_estimate=pl.CostEstimate(
            flops=2 * blocks * terms * width**3, bytes_accessed=9 * 2**20, transcendentals=0
        ),
        name="left_products",
    )(
        jnp.stack([own, me]).astype(jnp.int32),
        left_sector,
        term_mask,
        left_operators,
        wavefunction,
    )

    kept = []
    start = 0
    for number, columns in enumerate(WIDTHS):
        part = right_operators[:, :, start : start + columns, :]
        start += columns
        if owners <= RING_LIMIT and owners % 2 == 0:
            chips = owners // 2
            forward_steps = chips // 2 - number % 2
            pieces, table = ring_gather(part, forward_steps, chips)
        else:
            whole = lax.all_gather(part, "sec", axis=1, tiled=True)
            pieces, table = [whole], np.zeros((owners, 1), np.int32)
        pack = width // columns
        groups = blocks // pack
        partial = pl.pallas_call(
            functools.partial(right_kernel, pieces=len(pieces), parties=parties),
            out_shape=[jax.ShapeDtypeStruct((groups, rows, width), jnp.bfloat16)] * parties,
            in_specs=[smem, smem, vmem] + [anywhere] * len(pieces),
            out_specs=[vmem] * parties,
            scratch_shapes=[
                pltpu.VMEM((terms, owners * sectors, columns, width), jnp.bfloat16),
                pltpu.SemaphoreType.DMA((len(pieces),)),
            ],
            compiler_params=params,
            cost_estimate=pl.CostEstimate(
                flops=2 * blocks * terms * width**2 * columns,
                bytes_accessed=12 * 2**20,
                transcendentals=0,
            ),
            name="right_products",
        )(jnp.asarray(table)[me], right_sector, left_part, *pieces)
        kept.append(partial[0])
        for j in range(1, parties):
            turn = [(d, (d + j) % parties) for d in range(parties)]
            kept.append(lax.ppermute(partial[j], "mpo", turn))

    return pl.pallas_call(
        functools.partial(join_kernel, widths=WIDTHS, parties=parties),
        out_shape=jax.ShapeDtypeStruct((blocks, rows, width), jnp.bfloat16),
        in_specs=[vmem] * len(kept),
        out_specs=vmem,
        compiler_params=params,
        cost_estimate=pl.CostEstimate(flops=0, bytes_accessed=4 * 2**20, transcendentals=0),
        name="join_columns",
    )(*kept)


def solution(mesh):
    placed = (
        P("sec", None, None),
        P("sec"),
        P("sec"),
        P("mpo", "sec"),
        P("mpo", "sec", None, None),
        P("mpo", "sec", None, None),
    )
    return jax.shard_map(
        on_device, mesh=mesh, in_specs=placed, out_specs=P("sec", "mpo", None), check_vma=False
    )
```

```python
import functools

import jax
import jax.numpy as jnp
import numpy as np
from jax import lax
from jax.experimental import pallas as pl
from jax.experimental.pallas import tpu as pltpu
from jax.sharding import PartitionSpec as P

PLAN = "0P 0Q 0P 0Q La:0P 0Q Lb:0P 0Q:1P 0P:1Q 1P m0 m0:1Q 1P 1Q 1P y0:m1"
RING_LIMIT = 16
VMEM_LIMIT = 16 * 1024 * 1024
UNROLL = 10


def chip_ring(chips):
    across = 2 if chips % 2 == 0 else 1
    up = [z * across for z in range(chips // across)]
    down = [z * across + 1 for z in reversed(range(chips // across))] if across == 2 else []
    return up + down


def swap_cores(value, owners):
    return lax.ppermute(value, "sec", [(d, d ^ 1) for d in range(owners)])


def step_round(value, owners):
    order = chip_ring(owners // 2)
    after = {chip: order[(i + 1) % len(order)] for i, chip in enumerate(order)}
    before = {chip: order[i - 1] for i, chip in enumerate(order)}
    pairs = [(d, 2 * (after if d % 2 == 0 else before)[d // 2] + d % 2) for d in range(owners)]
    return lax.ppermute(value, "sec", pairs)


class RingGather:
    def __init__(self, part, owners):
        self.owners, self.chips = owners, owners // 2
        self.heads = [part, swap_cores(part, owners)]
        self.steps = [0, 0]
        self.pieces = list(self.heads)
        self.places = [(0, 0), (0, 1)]

    def rounds(self, lane):
        return self.chips // 2 if lane == 0 else (self.chips - 1) // 2

    def advance(self, lane, wait_for=()):
        head = self.heads[lane]
        if wait_for:
            head = lax.optimization_barrier((head, *wait_for))[0]
        head = step_round(head, self.owners)
        self.heads[lane] = head
        self.steps[lane] += 1
        self.pieces += [head, swap_cores(head, self.owners)]
        self.places += [(self.steps[lane], lane), (-self.steps[lane], 1 - lane)]

    def table(self):
        order = chip_ring(self.chips)
        place = {chip: i for i, chip in enumerate(order)}
        owners = np.zeros((self.owners, len(self.pieces)), np.int32)
        for d in range(self.owners):
            way = 1 if d % 2 else -1
            for number, (shift, other) in enumerate(self.places):
                chip = order[(place[d // 2] + way * shift) % self.chips]
                owners[d, number] = 2 * chip + (d % 2) ^ other
        return owners


def left_kernel(index_ref, operator_ref, wave_ref, out_ref, *, parties):
    terms, _, width, _ = operator_ref.shape
    blocks = wave_ref.shape[0]
    rows = width // parties
    own, before = index_ref[0], 1

    def one_block(b, carry):
        local = index_ref[before + b]
        bands = [
            operator_ref[k, local, pl.ds(pl.multiple_of(lax.rem(own + j, parties) * rows, rows), rows), :]
            for k in range(terms)
            for j in range(parties)
        ]
        product = jnp.dot(
            jnp.concatenate(bands, axis=0), wave_ref[b], preferred_element_type=jnp.float32
        )
        for k in range(terms):
            out_ref[b, :, k * width : (k + 1) * width] = product[
                k * width : (k + 1) * width
            ].astype(out_ref.dtype)
        return carry

    lax.fori_loop(0, blocks, one_block, 0, unroll=UNROLL)


def right_kernel(index_ref, *refs, lefts, pieces, parties):
    left_refs, refs = refs[:lefts], refs[lefts:]
    piece_refs, out_refs = refs[:pieces], refs[pieces : pieces + parties]
    held, arrived = refs[pieces + parties :]
    terms, total, columns, width = held.shape
    sectors = piece_refs[0].shape[1]
    blocks, height, _ = left_refs[0].shape
    rows = height // parties
    pack = width // columns
    before = pieces

    copies = [
        pltpu.make_async_copy(
            piece, held.at[:, pl.ds(index_ref[number] * sectors, sectors)], arrived.at[number]
        )
        for number, piece in enumerate(piece_refs)
    ]
    for copy in copies:
        copy.start()
    for copy in copies:
        copy.wait()
    lane = lax.broadcasted_iota(jnp.int32, (height, width), 1) // columns

    def one_group(g, carry):
        factors = []
        for q in range(pack):
            sector = index_ref[before + g * pack + q]
            factors.append(jnp.concatenate([held[k, sector] for k in range(terms)], axis=1))
        factor = jnp.concatenate(factors, axis=0)
        left = jnp.concatenate(
            [jnp.concatenate([ref[g * pack + q] for q in range(pack)], axis=0) for ref in left_refs],
            axis=1,
        )
        product = lax.dot_general(
            left, factor, (((1,), (1,)), ((), ())), preferred_element_type=jnp.float32
        ).reshape(pack, height, width)
        chosen = product[0]
        for q in range(1, pack):
            chosen = jnp.where(lane == q, product[q], chosen)
        for j in range(parties):
            out_refs[j][g] = chosen[j * rows : (j + 1) * rows].astype(out_refs[j].dtype)
        return carry

    lax.fori_loop(0, blocks // pack, one_group, 0, unroll=min(UNROLL, blocks // pack))


def join_kernel(own_ref, *refs, layout, parties):
    out_ref = refs[-1]
    blocks, rows, width = out_ref.shape
    most = max(width // columns for columns, _ in layout)
    lane = lax.broadcasted_iota(jnp.int32, (rows, width), 1)
    own = own_ref[0]

    def one_group(g, carry):
        bands = []
        for c, (columns, by_columns) in enumerate(layout):
            pack = width // columns
            given = refs[c * parties : (c + 1) * parties]
            inside = [[] for _ in range(parties if by_columns else 1)]
            for t in range(most // pack):
                values = [ref[g * (most // pack) + t].astype(jnp.float32) for ref in given]
                if by_columns:
                    inside[0].append(jnp.where(own == 0, values[0], values[1]))
                    inside[1].append(jnp.where(own == 0, values[1], values[0]))
                else:
                    total = values[0]
                    for other in values[1:]:
                        total = total + other
                    inside[0].append(total)
            bands += [(columns, packed) for packed in inside]
        for b in range(most):
            start, value = 0, None
            for columns, packed in bands:
                pack = width // columns
                turn = (start - (b % pack) * columns) % width
                moved = packed[b // pack]
                moved = pltpu.roll(moved, turn, 1) if turn else moved
                value = moved if value is None else jnp.where(lane >= start, moved, value)
                start += columns
            out_ref[g * most + b] = value.astype(out_ref.dtype)
        return carry

    lax.fori_loop(0, blocks // most, one_group, 0, unroll=4)


def follow_plan(rings, lefts, finish):
    done, results = dict(lefts), []
    for word in PLAN.split():
        wants, _, act = word.rpartition(":")
        others = [value for want in wants.split(",") if want for value in done[want]]
        if act[0] == "m":
            number = int(act[1])
            ring = rings[number]
            out, partial = finish(number, ring.pieces, ring.table(), others)
            results += out
            done[act], done["y" + act[1]] = partial, out[1:]
        else:
            ring, lane = rings[int(act[0])], "PQ".index(act[1])
            if ring.steps[lane] < ring.rounds(lane):
                ring.advance(lane, others)
            done[act] = [ring.heads[lane]]
    return results


def on_device(wavefunction, left_sector, right_sector, term_mask, left_operators, right_operators):
    owners, parties = lax.axis_size("sec"), lax.axis_size("mpo")
    me, own = lax.axis_index("sec"), lax.axis_index("mpo")
    terms, sectors, width, _ = left_operators.shape
    blocks = wavefunction.shape[0]
    rows, half = width // parties, width // 2
    smem = pl.BlockSpec(memory_space=pltpu.SMEM)
    vmem = pl.BlockSpec(memory_space=pltpu.VMEM)
    anywhere = pl.BlockSpec(memory_space=pl.ANY)
    params = pltpu.CompilerParams(vmem_limit_bytes=VMEM_LIMIT)

    def to_party(value, j):
        return lax.ppermute(value, "mpo", [(d, (d + j) % parties) for d in range(parties)])

    def left_products(operators):
        return pl.pallas_call(
            functools.partial(left_kernel, parties=parties),
            out_shape=jax.ShapeDtypeStruct((blocks, width, terms * width), jnp.bfloat16),
            in_specs=[smem, vmem, vmem],
            out_specs=vmem,
            compiler_params=params,
            cost_estimate=pl.CostEstimate(
                flops=2 * blocks * terms * width**3, bytes_accessed=9 * 2**20, transcendentals=0
            ),
            name="left_products",
        )(left_index, operators, wavefunction)

    def right_products(columns, lefts, pieces, table):
        pack = width // columns
        piece_terms = pieces[0].shape[0]
        index = jnp.concatenate([jnp.asarray(table)[me], right_sector])
        partial = pl.pallas_call(
            functools.partial(
                right_kernel, lefts=len(lefts), pieces=len(pieces), parties=parties
            ),
            out_shape=[jax.ShapeDtypeStruct((blocks // pack, rows, width), jnp.bfloat16)] * parties,
            in_specs=[smem] + [vmem] * len(lefts) + [anywhere] * len(pieces),
            out_specs=[vmem] * parties,
            scratch_shapes=[
                pltpu.VMEM((piece_terms, owners * sectors, columns, width), jnp.bfloat16),
                pltpu.SemaphoreType.DMA((len(pieces),)),
            ],
            compiler_params=params,
            cost_estimate=pl.CostEstimate(
                flops=2 * blocks * piece_terms * width**2 * columns,
                bytes_accessed=12 * 2**20,
                transcendentals=0,
            ),
            name="right_products",
        )(index, *lefts, *pieces)
        return [partial[0]] + [to_party(partial[j], j) for j in range(1, parties)], partial

    mask = term_mask.astype(left_operators.dtype)[:, :, None, None]
    masked = left_operators * mask
    left_index = jnp.concatenate([own[None], left_sector - me * sectors]).astype(jnp.int32)
    first = right_operators[:, :, :half, :]
    if parties == 2 and owners <= RING_LIMIT and owners % 2 == 0:
        quarter = half // 2
        others_masked = to_party(masked, 1)
        for_other = lax.dynamic_slice_in_dim(right_operators, half + quarter * (1 - own), quarter, 2)
        for_own = lax.dynamic_slice_in_dim(right_operators, half + quarter * own, quarter, 2)
        second = jnp.concatenate([for_own, to_party(for_other, 1)], axis=0)
        rings = [RingGather(first, owners), RingGather(second, owners)]
        lefts = [left_products(masked), left_products(others_masked)]
        layout = ((half, False), (quarter, True))

        def finish(number, pieces, table, others):
            if others:
                pieces = lax.optimization_barrier((*pieces, *others))[: len(pieces)]
            return right_products(layout[number][0], lefts[: number + 1], pieces, table)

        kept = follow_plan(rings, {"La": lefts[:1], "Lb": lefts[1:]}, finish)
    else:
        lefts = [left_products(masked)]
        layout = ((half, False), (width - half, False))
        kept = []
        for part in (first, right_operators[:, :, half:, :]):
            whole = lax.all_gather(part, "sec", axis=1, tiled=True)
            kept += right_products(part.shape[2], lefts, [whole], np.zeros((owners, 1), np.int32))[0]

    return pl.pallas_call(
        functools.partial(join_kernel, layout=layout, parties=parties),
        out_shape=jax.ShapeDtypeStruct((blocks, rows, width), jnp.bfloat16),
        in_specs=[smem] + [vmem] * len(kept),
        out_specs=vmem,
        compiler_params=params,
        cost_estimate=pl.CostEstimate(flops=0, bytes_accessed=4 * 2**20, transcendentals=0),
        name="join_columns",
    )(own[None].astype(jnp.int32), *kept)


def solution(mesh):
    placed = (
        P("sec", None, None),
        P("sec"),
        P("sec"),
        P("mpo", "sec"),
        P("mpo", "sec", None, None),
        P("mpo", "sec", None, None),
    )
    return jax.shard_map(
        on_device, mesh=mesh, in_specs=placed, out_specs=P("sec", "mpo", None), check_vma=False
    )
```

```python
import functools

import jax
import jax.numpy as jnp
import numpy as np
from jax import lax
from jax.experimental import pallas as pl
from jax.experimental.pallas import tpu as pltpu
from jax.sharding import PartitionSpec as P

RING_LIMIT = 16
VMEM_LIMIT = 24 * 1024 * 1024
UNROLL = 10
LEFT_BANDS = 4
JOIN_BANDS = 4
STAGES = ((0, 1, 2), (3,), (4,))
APART = 2
WAITS = {"P2o": ("masked",), "P1x": ("P2o",), "Q1x": ("Q2o",), "Q2o": ("given",), "Q2x": ("other",), "Q3": ("left",), "P4": ("m0",), "m2": ("y0",)}


def in_hbm(value):
    return pltpu.with_memory_space_constraint(value, pltpu.HBM)


def after(value, *others):
    return lax.optimization_barrier((value, *others))[0] if others else value


def chip_ring(chips):
    across = 2 if chips % 2 == 0 else 1
    up = [z * across for z in range(chips // across)]
    down = [z * across + 1 for z in reversed(range(chips // across))] if across == 2 else []
    return up + down


def swap_cores(value, owners):
    return lax.ppermute(value, "sec", [(d, d ^ 1) for d in range(owners)])


def step_round(value, owners):
    order = chip_ring(owners // 2)
    following = {chip: order[(i + 1) % len(order)] for i, chip in enumerate(order)}
    before = {chip: order[i - 1] for i, chip in enumerate(order)}
    pairs = [(d, 2 * (before if d % 2 else following)[d // 2] + d % 2) for d in range(owners)]
    return lax.ppermute(value, "sec", pairs)


def ring_rounds(owners):
    chips = owners // 2
    return chips // 2, (chips - 1) // 2


def ring_sources(owners, rounds):
    chips = owners // 2
    order = chip_ring(chips)
    place = {chip: i for i, chip in enumerate(order)}
    found = np.zeros((owners, 0), np.int32)
    for number in rounds:
        for lane, last in enumerate(ring_rounds(owners)):
            if number > last or (number == 0 and lane):
                continue
            for swapped in range(2):
                column = []
                for d in range(owners):
                    source = d ^ swapped
                    way = 1 if source % 2 else -1
                    chip = order[(place[d // 2] + way * number) % chips]
                    column.append(2 * chip + (source % 2) ^ lane)
                found = np.concatenate([found, np.array(column, np.int32)[:, None]], axis=1)
    return found


def left_kernel(index_ref, *refs, parties, count, base):
    operator_refs, wave_ref = refs[:count], refs[count]
    out_refs = refs[count + 1 : 2 * count + 1]
    operators, waves, arrived = refs[2 * count + 1 :]
    _, terms, _, width, _ = operators.shape
    blocks = waves.shape[0]
    rows = width // parties
    own = index_ref[0]
    copies = [
        pltpu.make_async_copy(ref, operators.at[n], arrived.at[n])
        for n, ref in enumerate(operator_refs)
    ]
    bands = blocks // LEFT_BANDS if blocks % LEFT_BANDS == 0 else blocks
    for n in range(blocks // bands):
        there = pl.ds(n * bands, bands)
        copies.append(
            pltpu.make_async_copy(wave_ref.at[there], waves.at[there], arrived.at[count + n])
        )
    for copy in copies:
        copy.start()
    for copy in copies[:count]:
        copy.wait()

    def one_block(b, carry):
        local = index_ref[base + b]
        strips = [
            operators[
                n, k, local, pl.ds(pl.multiple_of(lax.rem(own + j, parties) * rows, rows), rows), :
            ]
            for n in range(count)
            for k in range(terms)
            for j in range(parties)
        ]
        product = jnp.dot(
            jnp.concatenate(strips, axis=0), waves[b], preferred_element_type=jnp.float32
        ).astype(jnp.bfloat16)
        for n, out_ref in enumerate(out_refs):
            for k in range(terms):
                start = (n * terms + k) * width
                out_ref[b, :, k * width : (k + 1) * width] = product[start : start + width]
        return carry

    for n, copy in enumerate(copies[count:]):
        copy.wait()
        lax.fori_loop(n * bands, (n + 1) * bands, one_block, 0, unroll=UNROLL)


def right_kernel(index_ref, *refs, lefts, spots, parties, stage, bases):
    pieces = len(spots)
    left_refs, piece_refs = refs[:lefts], refs[lefts : lefts + pieces]
    out_refs = refs[lefts + pieces : lefts + pieces + parties]
    held, listed, arrived = refs[lefts + pieces + parties :]
    terms, _, columns, width = held.shape
    blocks, height, _ = left_refs[0].shape
    rows, pack = height // parties, width // columns
    slots = out_refs[0].shape[0] * pack
    shift_base, stage_base, target_base, sector_base = bases

    copies = []
    for number, (piece, (term, slot)) in enumerate(zip(piece_refs, spots)):
        there = held.at[pl.ds(term, piece.shape[0]), pl.ds(slot, piece.shape[1])]
        copies.append(pltpu.make_async_copy(piece, there, arrived.at[number]))
    for copy in copies:
        copy.start()
    if stage is not None:

        def clear(i, carry):
            listed[i] = 0
            return carry

        def enlist(b, count):
            listed[count] = b
            hit = index_ref[stage_base + index_ref[target_base + b]] == stage
            return count + hit.astype(jnp.int32)

        lax.fori_loop(0, slots + 1, clear, 0, unroll=True)
        lax.fori_loop(0, blocks, enlist, jnp.int32(0), unroll=10)
    for copy in copies:
        copy.wait()
    lane = lax.broadcasted_iota(jnp.int32, (height, width), 1) // columns

    def one_group(g, carry):
        chosen = [g * pack + q for q in range(pack)]
        if stage is not None:
            chosen = [listed[i] for i in chosen]
        factors = []
        for b in chosen:
            sector = index_ref[sector_base + b] + index_ref[shift_base + index_ref[target_base + b]]
            factors.append(jnp.concatenate([held[k, sector] for k in range(terms)], axis=1))
        left = jnp.concatenate(
            [jnp.concatenate([ref[b] for b in chosen], axis=0) for ref in left_refs], axis=1
        )
        product = lax.dot_general(
            left,
            jnp.concatenate(factors, axis=0),
            (((1,), (1,)), ((), ())),
            preferred_element_type=jnp.float32,
        ).reshape(pack, height, width)
        value = product[0]
        for q in range(1, pack):
            value = jnp.where(lane == q, product[q], value)
        for j in range(parties):
            out_refs[j][g] = value[j * rows : (j + 1) * rows].astype(out_refs[j].dtype)
        return carry

    lax.fori_loop(0, slots // pack, one_group, 0, unroll=min(UNROLL, slots // pack))


def join_kernel(index_ref, *refs, stages, bases):
    own_refs, other_refs = refs[:stages], refs[stages : 2 * stages]
    out_ref, joined, sent = refs[2 * stages :]
    blocks, rows, width = joined.shape
    stage_base, target_base = bases
    own = index_ref[0]
    upper = lax.broadcasted_iota(jnp.int32, (rows, width), 1) // (width // 2)

    def pick(given, places, stage):
        value = given[0][places[0]]
        for s in range(1, stages):
            value = jnp.where(stage == s, given[s][places[s]], value)
        return value.astype(jnp.float32)

    def one_block(b, counts):
        stage = index_ref[stage_base + index_ref[target_base + b]]
        slot, places, grown = b, [lax.shift_right_logical(b, 1)], []
        for s in range(1, stages):
            hit = stage == s
            slot = jnp.where(hit, counts[s - 1], slot)
            last = own_refs[s].shape[0] - 1
            places.append(jnp.minimum(lax.shift_right_logical(counts[s - 1], 1), last))
            grown.append(counts[s - 1] + hit.astype(jnp.int32))
        side = lax.bitwise_and(slot, 1)
        here = side == own
        mine, given = pick(own_refs, places, stage), pick(other_refs, places, stage)
        moved = pltpu.roll(jnp.where(here, given, mine), width // 2, 1)
        kept = jnp.where(here, mine, given)
        joined[b] = jnp.where(upper == side, kept, moved).astype(joined.dtype)
        return tuple(grown)

    counts = (jnp.int32(0),) * (stages - 1)
    bands = blocks // JOIN_BANDS if blocks % JOIN_BANDS == 0 else blocks
    copies = []
    for n in range(blocks // bands):
        counts = lax.fori_loop(n * bands, (n + 1) * bands, one_block, counts, unroll=10)
        there = pl.ds(n * bands, bands)
        copies.append(pltpu.make_async_copy(joined.at[there], out_ref.at[there], sent.at[n]))
        copies[-1].start()
    for copy in copies:
        copy.wait()


def on_device(wavefunction, left_sector, right_sector, term_mask, left_operators, right_operators):
    owners, parties = lax.axis_size("sec"), lax.axis_size("mpo")
    me, own = lax.axis_index("sec"), lax.axis_index("mpo")
    terms, sectors, width, _ = left_operators.shape
    blocks = wavefunction.shape[0]
    rows = width // parties
    smem = pl.BlockSpec(memory_space=pltpu.SMEM)
    vmem = pl.BlockSpec(memory_space=pltpu.VMEM)
    anywhere = pl.BlockSpec(memory_space=pl.ANY)
    params = pltpu.CompilerParams(vmem_limit_bytes=VMEM_LIMIT)
    by_ring = parties == 2 and owners <= RING_LIMIT and owners % 4 == 0 and blocks % 2 == 0

    def to_party(value, j):
        return lax.ppermute(value, "mpo", [(d, (d + j) % parties) for d in range(parties)])

    lanes = ring_rounds(owners) if by_ring else (0, 0)
    stages = [tuple(r for r in rounds if r <= lanes[0]) for rounds in STAGES] if by_ring else [(0,)]
    stages = [rounds for rounds in stages if rounds]
    sources = [ring_sources(owners, rounds) for rounds in stages] if by_ring else []
    shifts = np.zeros((owners, len(stages), owners), np.int32)
    stage_of = np.zeros((owners, owners), np.int32)
    for s, found in enumerate(sources):
        for d in range(owners):
            shifts[d, s] = -sectors * np.arange(owners)
            for slot, owner in enumerate(found[d]):
                shifts[d, s, owner] = sectors * (slot - owner)
                stage_of[d, owner] = s
    table = np.concatenate([shifts.reshape(owners, -1), stage_of], axis=1)
    stage_base = 1 + len(stages) * owners
    target_base = stage_base + owners
    sector_base = target_base + blocks
    left_base = sector_base + blocks
    index = jnp.concatenate(
        [
            own[None],
            jnp.asarray(table)[me],
            right_sector // sectors,
            right_sector,
            left_sector - me * sectors,
        ]
    ).astype(jnp.int32)

    def left_products(operators):
        return pl.pallas_call(
            functools.partial(
                left_kernel, parties=parties, count=len(operators), base=left_base
            ),
            out_shape=[jax.ShapeDtypeStruct((blocks, width, terms * width), jnp.bfloat16)]
            * len(operators),
            in_specs=[smem] + [anywhere] * (len(operators) + 1),
            out_specs=[vmem] * len(operators),
            scratch_shapes=[
                pltpu.VMEM((len(operators), *operators[0].shape), jnp.bfloat16),
                pltpu.VMEM(wavefunction.shape, jnp.bfloat16),
                pltpu.SemaphoreType.DMA((len(operators) + LEFT_BANDS,)),
            ],
            compiler_params=params,
            cost_estimate=pl.CostEstimate(
                flops=2 * len(operators) * blocks * terms * width**3,
                bytes_accessed=9 * 2**20,
                transcendentals=0,
            ),
            name="left_products",
        )(index, *operators, in_hbm(wavefunction))

    def right_products(lefts, pieces, spots, stage, held, slots):
        pack = width // held[2]
        return pl.pallas_call(
            functools.partial(
                right_kernel,
                lefts=len(lefts),
                spots=spots,
                parties=parties,
                stage=stage or None,
                bases=(1 + (stage or 0) * owners, stage_base, target_base, sector_base),
            ),
            out_shape=[jax.ShapeDtypeStruct((slots // pack, rows, width), jnp.bfloat16)] * parties,
            in_specs=[smem] + [vmem] * len(lefts) + [anywhere] * len(pieces),
            out_specs=[vmem] * parties,
            scratch_shapes=[
                pltpu.VMEM(held, jnp.bfloat16),
                pltpu.SMEM((slots + 1,), jnp.int32),
                pltpu.SemaphoreType.DMA((len(pieces),)),
            ],
            compiler_params=params,
            cost_estimate=pl.CostEstimate(
                flops=2 * slots * held[0] * width**2 * held[2],
                bytes_accessed=12 * 2**20,
                transcendentals=0,
            ),
            name="right_products",
        )(index, *lefts, *pieces)

    mask = term_mask.astype(left_operators.dtype)[:, :, None, None]
    masked = left_operators * mask
    if not by_ring:
        lefts = left_products([masked])
        whole = lax.all_gather(right_operators, "sec", axis=1, tiled=True)
        shape = (terms, owners * sectors, width, width)
        partial = right_products(lefts, [whole], [(0, 0)], None, shape, blocks)
        total = partial[0].astype(jnp.float32)
        for j in range(1, parties):
            total = total + to_party(partial[j], j).astype(jnp.float32)
        return total.astype(jnp.bfloat16)

    columns = width // parties
    mine = lax.dynamic_slice_in_dim(right_operators, columns * own, columns, 2)
    theirs = lax.dynamic_slice_in_dim(right_operators, columns * (1 - own), columns, 2)
    given = to_party(theirs, 1)
    other = to_party(masked, 1)
    lefts = left_products([masked, other])
    done = {"given": [given], "other": [other], "left": lefts, "masked": [masked]}

    def launch(name, value):
        waits = [v for w in WAITS.get(name, ()) for v in done[w]]
        done[name] = [step_round(after(value, *waits), owners)]
        return done[name][0]

    trails = []
    for n, part in enumerate((mine, given)):
        heads = [part, swap_cores(part, owners)]
        trail = {(0, 0): heads[0], (0, 1): heads[1]}
        for number in range(1, APART + 1):
            for lane in range(2):
                if number <= lanes[lane]:
                    heads[lane] = launch("PQ"[lane] + str(number) + "ox"[n], heads[lane])
                    trail[number, lane] = heads[lane]
        trails.append(trail)
    joined = {}
    kept = []
    for s, rounds in enumerate(stages):
        gathered, spots, count = [], [], 0
        for number in rounds:
            for lane in range(2):
                if number > lanes[lane] or (number == 0 and lane):
                    continue
                if number == 0:
                    found = [(n * terms, trail[0, q], q) for n, trail in enumerate(trails) for q in range(2)]
                elif number <= APART:
                    found = [
                        (n * terms, v, q)
                        for n, trail in enumerate(trails)
                        for q, v in enumerate((trail[number, lane], swap_cores(trail[number, lane], owners)))
                    ]
                else:
                    if lane not in joined:
                        joined[lane] = jnp.concatenate([trail[APART, lane] for trail in trails], axis=0)
                    head = joined[lane] = launch("PQ"[lane] + str(number), joined[lane])
                    found = [(0, head, 0), (0, swap_cores(head, owners), 1)]
                for term, piece, q in found:
                    gathered.append(piece)
                    spots.append((term, (count + q) * sectors))
                count += 2
        waits = [v for w in WAITS.get("m" + str(s), ()) for v in done[w]]
        gathered[0] = after(gathered[0], *waits)
        slots = blocks if s == 0 else min(blocks, count * sectors)
        held = (parties * terms, count * sectors, columns, width)
        partial = right_products(lefts, gathered, spots, s, held, slots)
        done["m" + str(s)] = partial
        done["y" + str(s)] = [to_party(partial[1], 1)]
        kept.append((partial[0], done["y" + str(s)][0]))

    return pl.pallas_call(
        functools.partial(join_kernel, stages=len(kept), bases=(stage_base, target_base)),
        out_shape=jax.ShapeDtypeStruct((blocks, rows, width), jnp.bfloat16),
        in_specs=[smem] + [vmem] * (2 * len(kept)),
        out_specs=anywhere,
        scratch_shapes=[
            pltpu.VMEM((blocks, rows, width), jnp.bfloat16),
            pltpu.SemaphoreType.DMA((JOIN_BANDS,)),
        ],
        compiler_params=params,
        cost_estimate=pl.CostEstimate(flops=0, bytes_accessed=4 * 2**20, transcendentals=0),
        name="join_columns",
    )(index, *[pair[0] for pair in kept], *[pair[1] for pair in kept])


def solution(mesh):
    placed = (
        P("sec", None, None),
        P("sec"),
        P("sec"),
        P("mpo", "sec"),
        P("mpo", "sec", None, None),
        P("mpo", "sec", None, None),
    )
    return jax.shard_map(
        on_device, mesh=mesh, in_specs=placed, out_specs=P("sec", "mpo", None), check_vma=False
    )
```

```python
import functools

import jax
import jax.numpy as jnp
import numpy as np
from jax import lax
from jax.experimental import pallas as pl
from jax.experimental.pallas import tpu as pltpu
from jax.sharding import PartitionSpec as P

RING_LIMIT = 16
VMEM_LIMIT = 24 * 1024 * 1024
UNROLL = 10
LEFT_BANDS = 4
JOIN_BANDS = 4
STAGES = ((0, 1, 2), (3,), (4,))
APART = 2
WAITS = {"P2o": ('masked',), "P1x": ('P2o',), "Q1x": ('Q2o',), "Q2o": ('given',), "P4": ('m0',), "P2x": ('index', 'other'), "P3": ('Q2x', 'left'), "m1": ('y0',)}


def in_hbm(value):
    return pltpu.with_memory_space_constraint(value, pltpu.HBM)


def after(value, *others):
    return lax.optimization_barrier((value, *others))[0] if others else value


def chip_ring(chips):
    across = 2 if chips % 2 == 0 else 1
    up = [z * across for z in range(chips // across)]
    down = [z * across + 1 for z in reversed(range(chips // across))] if across == 2 else []
    return up + down


def swap_cores(value, owners):
    return lax.ppermute(value, "sec", [(d, d ^ 1) for d in range(owners)])


def step_round(value, owners):
    order = chip_ring(owners // 2)
    following = {chip: order[(i + 1) % len(order)] for i, chip in enumerate(order)}
    before = {chip: order[i - 1] for i, chip in enumerate(order)}
    pairs = [(d, 2 * (before if d % 2 else following)[d // 2] + d % 2) for d in range(owners)]
    return lax.ppermute(value, "sec", pairs)


def ring_rounds(owners):
    chips = owners // 2
    return chips // 2, (chips - 1) // 2


def ring_sources(owners, rounds):
    chips = owners // 2
    order = chip_ring(chips)
    place = {chip: i for i, chip in enumerate(order)}
    found = np.zeros((owners, 0), np.int32)
    for number in rounds:
        for lane, last in enumerate(ring_rounds(owners)):
            if number > last or (number == 0 and lane):
                continue
            for swapped in range(2):
                column = []
                for d in range(owners):
                    source = d ^ swapped
                    way = 1 if source % 2 else -1
                    chip = order[(place[d // 2] + way * number) % chips]
                    column.append(2 * chip + (source % 2) ^ lane)
                found = np.concatenate([found, np.array(column, np.int32)[:, None]], axis=1)
    return found


def left_kernel(index_ref, *refs, parties, count, base):
    operator_refs, wave_ref = refs[:count], refs[count]
    out_refs = refs[count + 1 : 2 * count + 1]
    operators, waves, arrived = refs[2 * count + 1 :]
    _, terms, _, width, _ = operators.shape
    blocks = waves.shape[0]
    rows = width // parties
    own = index_ref[0]
    copies = [
        pltpu.make_async_copy(ref, operators.at[n], arrived.at[n])
        for n, ref in enumerate(operator_refs)
    ]
    bands = blocks // LEFT_BANDS if blocks % LEFT_BANDS == 0 else blocks
    for n in range(blocks // bands):
        there = pl.ds(n * bands, bands)
        copies.append(
            pltpu.make_async_copy(wave_ref.at[there], waves.at[there], arrived.at[count + n])
        )
    for copy in copies[: count + 1]:
        copy.start()
    for copy in copies[:count]:
        copy.wait()
    for copy in copies[count + 1 :]:
        copy.start()

    def one_block(b, carry):
        local = index_ref[base + b]
        strips = [
            operators[
                n, k, local, pl.ds(pl.multiple_of(lax.rem(own + j, parties) * rows, rows), rows), :
            ]
            for n in range(count)
            for k in range(terms)
            for j in range(parties)
        ]
        product = jnp.dot(
            jnp.concatenate(strips, axis=0), waves[b], preferred_element_type=jnp.float32
        ).astype(jnp.bfloat16)
        for n, out_ref in enumerate(out_refs):
            for k in range(terms):
                start = (n * terms + k) * width
                out_ref[b, :, k * width : (k + 1) * width] = product[start : start + width]
        return carry

    for n, copy in enumerate(copies[count:]):
        copy.wait()
        lax.fori_loop(n * bands, (n + 1) * bands, one_block, 0, unroll=2 * UNROLL)


def right_kernel(index_ref, *refs, lefts, spots, parties, stage, bases):
    pieces = len(spots)
    left_refs, piece_refs = refs[:lefts], refs[lefts : lefts + pieces]
    out_refs = refs[lefts + pieces : lefts + pieces + parties]
    held, listed, arrived = refs[lefts + pieces + parties :]
    terms, _, columns, width = held.shape
    blocks, height, _ = left_refs[0].shape
    rows, pack = height // parties, width // columns
    slots = out_refs[0].shape[0] * pack
    shift_base, stage_base, target_base, sector_base = bases

    copies = []
    for number, (piece, (term, slot)) in enumerate(zip(piece_refs, spots)):
        there = held.at[pl.ds(term, piece.shape[0]), pl.ds(slot, piece.shape[1])]
        copies.append(pltpu.make_async_copy(piece, there, arrived.at[number]))
    for copy in copies:
        copy.start()
    if stage is not None:

        def clear(i, carry):
            listed[i] = 0
            return carry

        def enlist(b, count):
            listed[count] = b
            hit = index_ref[stage_base + index_ref[target_base + b]] == stage
            return count + hit.astype(jnp.int32)

        lax.fori_loop(0, slots + 1, clear, 0, unroll=True)
        lax.fori_loop(0, blocks, enlist, jnp.int32(0), unroll=10)
    for copy in copies:
        copy.wait()
    lane = lax.broadcasted_iota(jnp.int32, (height, width), 1) // columns

    def one_group(g, carry):
        chosen = [g * pack + q for q in range(pack)]
        if stage is not None:
            chosen = [listed[i] for i in chosen]
        factors = []
        for b in chosen:
            sector = index_ref[sector_base + b] + index_ref[shift_base + index_ref[target_base + b]]
            factors.append(jnp.concatenate([held[k, sector] for k in range(terms)], axis=1))
        left = jnp.concatenate(
            [jnp.concatenate([ref[b] for b in chosen], axis=0) for ref in left_refs], axis=1
        )
        product = lax.dot_general(
            left,
            jnp.concatenate(factors, axis=0),
            (((1,), (1,)), ((), ())),
            preferred_element_type=jnp.float32,
        ).reshape(pack, height, width)
        value = product[0]
        for q in range(1, pack):
            value = jnp.where(lane == q, product[q], value)
        for j in range(parties):
            out_refs[j][g] = value[j * rows : (j + 1) * rows].astype(out_refs[j].dtype)
        return carry

    lax.fori_loop(0, slots // pack, one_group, 0, unroll=min(2 * UNROLL, slots // pack))


def join_kernel(index_ref, *refs, stages, bases):
    own_refs, other_refs = refs[:stages], refs[stages : 2 * stages]
    out_ref, joined, sent = refs[2 * stages :]
    blocks, rows, width = joined.shape
    stage_base, target_base = bases
    own = index_ref[0]
    upper = lax.broadcasted_iota(jnp.int32, (rows, width), 1) // (width // 2)

    def pick(given, places, stage):
        value = given[0][places[0]]
        for s in range(1, stages):
            value = jnp.where(stage == s, given[s][places[s]], value)
        return value.astype(jnp.float32)

    def one_block(b, counts):
        stage = index_ref[stage_base + index_ref[target_base + b]]
        slot, places, grown = b, [lax.shift_right_logical(b, 1)], []
        for s in range(1, stages):
            hit = stage == s
            slot = jnp.where(hit, counts[s - 1], slot)
            last = own_refs[s].shape[0] - 1
            places.append(jnp.minimum(lax.shift_right_logical(counts[s - 1], 1), last))
            grown.append(counts[s - 1] + hit.astype(jnp.int32))
        side = lax.bitwise_and(slot, 1)
        here = side == own
        mine, given = pick(own_refs, places, stage), pick(other_refs, places, stage)
        moved = pltpu.roll(jnp.where(here, given, mine), width // 2, 1)
        kept = jnp.where(here, mine, given)
        joined[b] = jnp.where(upper == side, kept, moved).astype(joined.dtype)
        return tuple(grown)

    counts = (jnp.int32(0),) * (stages - 1)
    bands = blocks // JOIN_BANDS if blocks % JOIN_BANDS == 0 else blocks
    copies = []
    for n in range(blocks // bands):
        counts = lax.fori_loop(n * bands, (n + 1) * bands, one_block, counts, unroll=10)
        there = pl.ds(n * bands, bands)
        copies.append(pltpu.make_async_copy(joined.at[there], out_ref.at[there], sent.at[n]))
        copies[-1].start()
    for copy in copies:
        copy.wait()


def on_device(wavefunction, left_sector, right_sector, term_mask, left_operators, right_operators):
    owners, parties = lax.axis_size("sec"), lax.axis_size("mpo")
    me, own = lax.axis_index("sec"), lax.axis_index("mpo")
    terms, sectors, width, _ = left_operators.shape
    blocks = wavefunction.shape[0]
    rows = width // parties
    smem = pl.BlockSpec(memory_space=pltpu.SMEM)
    vmem = pl.BlockSpec(memory_space=pltpu.VMEM)
    anywhere = pl.BlockSpec(memory_space=pl.ANY)
    params = pltpu.CompilerParams(vmem_limit_bytes=VMEM_LIMIT)
    by_ring = parties == 2 and owners <= RING_LIMIT and owners % 4 == 0 and blocks % 2 == 0

    def to_party(value, j):
        return lax.ppermute(value, "mpo", [(d, (d + j) % parties) for d in range(parties)])

    lanes = ring_rounds(owners) if by_ring else (0, 0)
    stages = [tuple(r for r in rounds if r <= lanes[0]) for rounds in STAGES] if by_ring else [(0,)]
    stages = [rounds for rounds in stages if rounds]
    sources = [ring_sources(owners, rounds) for rounds in stages] if by_ring else []
    shifts = np.zeros((owners, len(stages), owners), np.int32)
    stage_of = np.zeros((owners, owners), np.int32)
    for s, found in enumerate(sources):
        for d in range(owners):
            shifts[d, s] = -sectors * np.arange(owners)
            for slot, owner in enumerate(found[d]):
                shifts[d, s, owner] = sectors * (slot - owner)
                stage_of[d, owner] = s
    table = np.concatenate([shifts.reshape(owners, -1), stage_of], axis=1)
    stage_base = 1 + len(stages) * owners
    target_base = stage_base + owners
    sector_base = target_base + blocks
    left_base = sector_base + blocks
    index = jnp.concatenate(
        [
            own[None],
            jnp.asarray(table)[me],
            right_sector // sectors,
            right_sector,
            left_sector - me * sectors,
        ]
    ).astype(jnp.int32)

    def left_products(operators):
        return pl.pallas_call(
            functools.partial(
                left_kernel, parties=parties, count=len(operators), base=left_base
            ),
            out_shape=[jax.ShapeDtypeStruct((blocks, width, terms * width), jnp.bfloat16)]
            * len(operators),
            in_specs=[smem] + [anywhere] * (len(operators) + 1),
            out_specs=[vmem] * len(operators),
            scratch_shapes=[
                pltpu.VMEM((len(operators), *operators[0].shape), jnp.bfloat16),
                pltpu.VMEM(wavefunction.shape, jnp.bfloat16),
                pltpu.SemaphoreType.DMA((len(operators) + LEFT_BANDS,)),
            ],
            compiler_params=params,
            cost_estimate=pl.CostEstimate(
                flops=2 * len(operators) * blocks * terms * width**3,
                bytes_accessed=9 * 2**20,
                transcendentals=0,
            ),
            name="left_products",
        )(index, *operators, in_hbm(wavefunction))

    def right_products(lefts, pieces, spots, stage, held, slots):
        pack = width // held[2]
        return pl.pallas_call(
            functools.partial(
                right_kernel,
                lefts=len(lefts),
                spots=spots,
                parties=parties,
                stage=stage or None,
                bases=(1 + (stage or 0) * owners, stage_base, target_base, sector_base),
            ),
            out_shape=[jax.ShapeDtypeStruct((slots // pack, rows, width), jnp.bfloat16)] * parties,
            in_specs=[smem] + [vmem] * len(lefts) + [anywhere] * len(pieces),
            out_specs=[vmem] * parties,
            scratch_shapes=[
                pltpu.VMEM(held, jnp.bfloat16),
                pltpu.SMEM((slots + 1,), jnp.int32),
                pltpu.SemaphoreType.DMA((len(pieces),)),
            ],
            compiler_params=params,
            cost_estimate=pl.CostEstimate(
                flops=2 * slots * held[0] * width**2 * held[2],
                bytes_accessed=12 * 2**20,
                transcendentals=0,
            ),
            name="right_products",
        )(index, *lefts, *pieces)

    mask = term_mask.astype(left_operators.dtype)[:, :, None, None]
    masked = left_operators * mask
    if not by_ring:
        lefts = left_products([masked])
        whole = lax.all_gather(right_operators, "sec", axis=1, tiled=True)
        shape = (terms, owners * sectors, width, width)
        partial = right_products(lefts, [whole], [(0, 0)], None, shape, blocks)
        total = partial[0].astype(jnp.float32)
        for j in range(1, parties):
            total = total + to_party(partial[j], j).astype(jnp.float32)
        return total.astype(jnp.bfloat16)

    columns = width // parties
    mine = lax.dynamic_slice_in_dim(right_operators, columns * own, columns, 2)
    theirs = lax.dynamic_slice_in_dim(right_operators, columns * (1 - own), columns, 2)
    given = to_party(theirs, 1)
    other = to_party(masked, 1)
    lefts = left_products([masked, other])
    done = {"given": [given], "other": [other], "left": lefts, "masked": [masked], "index": [index]}

    def launch(name, value):
        waits = [v for w in WAITS.get(name, ()) for v in done[w]]
        done[name] = [step_round(after(value, *waits), owners)]
        return done[name][0]

    trails = []
    for n, part in enumerate((mine, given)):
        heads = [part, swap_cores(part, owners)]
        trail = {(0, 0): heads[0], (0, 1): heads[1]}
        for number in range(1, APART + 1):
            for lane in range(2):
                if number <= lanes[lane]:
                    heads[lane] = launch("PQ"[lane] + str(number) + "ox"[n], heads[lane])
                    trail[number, lane] = heads[lane]
        trails.append(trail)
    joined = {}
    kept = []
    for s, rounds in enumerate(stages):
        gathered, spots, count = [], [], 0
        for number in rounds:
            for lane in range(2):
                if number > lanes[lane] or (number == 0 and lane):
                    continue
                if number == 0:
                    found = [(n * terms, trail[0, q], q) for n, trail in enumerate(trails) for q in range(2)]
                elif number <= APART:
                    found = [
                        (n * terms, v, q)
                        for n, trail in enumerate(trails)
                        for q, v in enumerate((trail[number, lane], swap_cores(trail[number, lane], owners)))
                    ]
                else:
                    if lane not in joined:
                        joined[lane] = jnp.concatenate([trail[APART, lane] for trail in trails], axis=0)
                    head = joined[lane] = launch("PQ"[lane] + str(number), joined[lane])
                    waits = [v for w in WAITS.get("S" + str(number) + "PQ"[lane], ()) for v in done[w]]
                    found = [(0, head, 0), (0, swap_cores(after(head, *waits), owners), 1)]
                for term, piece, q in found:
                    gathered.append(piece)
                    spots.append((term, (count + q) * sectors))
                count += 2
        waits = [v for w in WAITS.get("m" + str(s), ()) for v in done[w]]
        gathered[0] = after(gathered[0], *waits)
        slots = blocks if s == 0 else min(blocks, count * sectors)
        held = (parties * terms, count * sectors, columns, width)
        partial = right_products(lefts, gathered, spots, s, held, slots)
        done["m" + str(s)] = partial
        done["y" + str(s)] = [to_party(partial[1], 1)]
        kept.append((partial[0], done["y" + str(s)][0]))

    return pl.pallas_call(
        functools.partial(join_kernel, stages=len(kept), bases=(stage_base, target_base)),
        out_shape=jax.ShapeDtypeStruct((blocks, rows, width), jnp.bfloat16),
        in_specs=[smem] + [vmem] * (2 * len(kept)),
        out_specs=anywhere,
        scratch_shapes=[
            pltpu.VMEM((blocks, rows, width), jnp.bfloat16),
            pltpu.SemaphoreType.DMA((JOIN_BANDS,)),
        ],
        compiler_params=params,
        cost_estimate=pl.CostEstimate(flops=0, bytes_accessed=4 * 2**20, transcendentals=0),
        name="join_columns",
    )(index, *[pair[0] for pair in kept], *[pair[1] for pair in kept])


def solution(mesh):
    placed = (
        P("sec", None, None),
        P("sec"),
        P("sec"),
        P("mpo", "sec"),
        P("mpo", "sec", None, None),
        P("mpo", "sec", None, None),
    )
    return jax.shard_map(
        on_device, mesh=mesh, in_specs=placed, out_specs=P("sec", "mpo", None), check_vma=False
    )
```

```python
import functools

import jax
import jax.numpy as jnp
import numpy as np
from jax import lax
from jax.experimental import pallas as pl
from jax.experimental.pallas import tpu as pltpu
from jax.sharding import PartitionSpec as P

RING_LIMIT = 16
VMEM_LIMIT = 24 * 1024 * 1024
UNROLL = 10
LEFT_BANDS = 5
JOIN_BANDS = 4
STAGES = ((0, 1, 2), (3,), (4,))
APART = 2
WAITS = {"P2o": ('masked',), "P1x": ('P2o',), "Q1x": ('Q2o',), "P2x": ('index', 'other'), "P3": ('Q2x', 'left'), "P4": ('m0',), "m1": ('y0',)}


def in_hbm(value):
    return pltpu.with_memory_space_constraint(value, pltpu.HBM)


def after(value, *others):
    return lax.optimization_barrier((value, *others))[0] if others else value


def chip_ring(chips):
    across = 2 if chips % 2 == 0 else 1
    up = [z * across for z in range(chips // across)]
    down = [z * across + 1 for z in reversed(range(chips // across))] if across == 2 else []
    return up + down


def swap_cores(value, owners):
    return lax.ppermute(value, "sec", [(d, d ^ 1) for d in range(owners)])


def step_round(value, owners):
    order = chip_ring(owners // 2)
    following = {chip: order[(i + 1) % len(order)] for i, chip in enumerate(order)}
    before = {chip: order[i - 1] for i, chip in enumerate(order)}
    pairs = [(d, 2 * (before if d % 2 else following)[d // 2] + d % 2) for d in range(owners)]
    return lax.ppermute(value, "sec", pairs)


def ring_rounds(owners):
    chips = owners // 2
    return chips // 2, (chips - 1) // 2


def ring_sources(owners, rounds):
    chips = owners // 2
    order = chip_ring(chips)
    place = {chip: i for i, chip in enumerate(order)}
    found = np.zeros((owners, 0), np.int32)
    for number in rounds:
        for lane, last in enumerate(ring_rounds(owners)):
            if number > last or (number == 0 and lane):
                continue
            for swapped in range(2):
                column = []
                for d in range(owners):
                    source = d ^ swapped
                    way = 1 if source % 2 else -1
                    chip = order[(place[d // 2] + way * number) % chips]
                    column.append(2 * chip + (source % 2) ^ lane)
                found = np.concatenate([found, np.array(column, np.int32)[:, None]], axis=1)
    return found


def left_kernel(index_ref, *refs, parties, count, base):
    operator_refs, wave_ref = refs[:count], refs[count]
    out_refs = refs[count + 1 : 2 * count + 1]
    operators, waves, arrived = refs[2 * count + 1 :]
    _, terms, _, width, _ = operators.shape
    blocks = waves.shape[0]
    rows = width // parties
    own = index_ref[0]
    copies = [
        pltpu.make_async_copy(ref, operators.at[n], arrived.at[n])
        for n, ref in enumerate(operator_refs)
    ]
    bands = blocks // LEFT_BANDS if blocks % LEFT_BANDS == 0 else blocks
    for n in range(blocks // bands):
        there = pl.ds(n * bands, bands)
        copies.append(
            pltpu.make_async_copy(wave_ref.at[there], waves.at[there], arrived.at[count + n])
        )
    for copy in copies[: count + 1]:
        copy.start()
    for copy in copies[:count]:
        copy.wait()
    for copy in copies[count + 1 :]:
        copy.start()

    def one_block(b, carry):
        local = index_ref[base + b]
        strips = [
            operators[
                n, k, local, pl.ds(pl.multiple_of(lax.rem(own + j, parties) * rows, rows), rows), :
            ]
            for n in range(count)
            for k in range(terms)
            for j in range(parties)
        ]
        product = jnp.dot(
            jnp.concatenate(strips, axis=0), waves[b], preferred_element_type=jnp.float32
        ).astype(jnp.bfloat16)
        for n, out_ref in enumerate(out_refs):
            for k in range(terms):
                start = (n * terms + k) * width
                out_ref[b, :, k * width : (k + 1) * width] = product[start : start + width]
        return carry

    for n, copy in enumerate(copies[count:]):
        copy.wait()
        lax.fori_loop(n * bands, (n + 1) * bands, one_block, 0, unroll=16)


def right_kernel(index_ref, *refs, lefts, spots, parties, stage, bases):
    pieces = len(spots)
    left_refs, piece_refs = refs[:lefts], refs[lefts : lefts + pieces]
    out_refs = refs[lefts + pieces : lefts + pieces + parties]
    held, listed, arrived = refs[lefts + pieces + parties :]
    terms, _, columns, width = held.shape
    blocks, height, _ = left_refs[0].shape
    rows, pack = height // parties, width // columns
    slots = out_refs[0].shape[0] * pack
    shift_base, stage_base, target_base, sector_base = bases

    copies = []
    for number, (piece, (term, slot)) in enumerate(zip(piece_refs, spots)):
        there = held.at[pl.ds(term, piece.shape[0]), pl.ds(slot, piece.shape[1])]
        copies.append(pltpu.make_async_copy(piece, there, arrived.at[number]))
    for copy in copies:
        copy.start()
    if stage is not None:

        def clear(i, carry):
            listed[i] = 0
            return carry

        def enlist(b, count):
            listed[count] = b
            hit = index_ref[stage_base + index_ref[target_base + b]] == stage
            return count + hit.astype(jnp.int32)

        lax.fori_loop(0, slots + 1, clear, 0, unroll=True)
        lax.fori_loop(0, blocks, enlist, jnp.int32(0), unroll=10)
    for copy in copies:
        copy.wait()
    lane = lax.broadcasted_iota(jnp.int32, (height, width), 1) // columns

    def one_group(g, carry):
        chosen = [g * pack + q for q in range(pack)]
        if stage is not None:
            chosen = [listed[i] for i in chosen]
        factors = []
        for b in chosen:
            sector = index_ref[sector_base + b] + index_ref[shift_base + index_ref[target_base + b]]
            factors.append(jnp.concatenate([held[k, sector] for k in range(terms)], axis=1))
        left = jnp.concatenate(
            [jnp.concatenate([ref[b] for b in chosen], axis=0) for ref in left_refs], axis=1
        )
        product = lax.dot_general(
            left,
            jnp.concatenate(factors, axis=0),
            (((1,), (1,)), ((), ())),
            preferred_element_type=jnp.float32,
        ).reshape(pack, height, width)
        value = product[0]
        for q in range(1, pack):
            value = jnp.where(lane == q, product[q], value)
        for j in range(parties):
            out_refs[j][g] = value[j * rows : (j + 1) * rows].astype(out_refs[j].dtype)
        return carry

    lax.fori_loop(0, slots // pack, one_group, 0, unroll=min(4 * UNROLL, slots // pack))


def join_kernel(index_ref, *refs, stages, bases):
    own_refs, other_refs = refs[:stages], refs[stages : 2 * stages]
    out_ref, joined, sent = refs[2 * stages :]
    blocks, rows, width = joined.shape
    stage_base, target_base = bases
    own = index_ref[0]
    upper = lax.broadcasted_iota(jnp.int32, (rows, width), 1) // (width // 2)

    def pick(given, places, stage):
        value = given[0][places[0]]
        for s in range(1, stages):
            value = jnp.where(stage == s, given[s][places[s]], value)
        return value.astype(jnp.float32)

    def one_block(b, counts):
        stage = index_ref[stage_base + index_ref[target_base + b]]
        slot, places, grown = b, [lax.shift_right_logical(b, 1)], []
        for s in range(1, stages):
            hit = stage == s
            slot = jnp.where(hit, counts[s - 1], slot)
            last = own_refs[s].shape[0] - 1
            places.append(jnp.minimum(lax.shift_right_logical(counts[s - 1], 1), last))
            grown.append(counts[s - 1] + hit.astype(jnp.int32))
        side = lax.bitwise_and(slot, 1)
        here = side == own
        mine, given = pick(own_refs, places, stage), pick(other_refs, places, stage)
        moved = pltpu.roll(jnp.where(here, given, mine), width // 2, 1)
        kept = jnp.where(here, mine, given)
        joined[b] = jnp.where(upper == side, kept, moved).astype(joined.dtype)
        return tuple(grown)

    counts = (jnp.int32(0),) * (stages - 1)
    bands = blocks // JOIN_BANDS if blocks % JOIN_BANDS == 0 else blocks
    copies = []
    for n in range(blocks // bands):
        counts = lax.fori_loop(n * bands, (n + 1) * bands, one_block, counts, unroll=20)
        there = pl.ds(n * bands, bands)
        copies.append(pltpu.make_async_copy(joined.at[there], out_ref.at[there], sent.at[n]))
        copies[-1].start()
    for copy in copies:
        copy.wait()


def on_device(wavefunction, left_sector, right_sector, term_mask, left_operators, right_operators):
    owners, parties = lax.axis_size("sec"), lax.axis_size("mpo")
    me, own = lax.axis_index("sec"), lax.axis_index("mpo")
    terms, sectors, width, _ = left_operators.shape
    blocks = wavefunction.shape[0]
    rows = width // parties
    smem = pl.BlockSpec(memory_space=pltpu.SMEM)
    vmem = pl.BlockSpec(memory_space=pltpu.VMEM)
    anywhere = pl.BlockSpec(memory_space=pl.ANY)
    params = pltpu.CompilerParams(vmem_limit_bytes=VMEM_LIMIT)
    by_ring = parties == 2 and owners <= RING_LIMIT and owners % 4 == 0 and blocks % 2 == 0

    def to_party(value, j):
        return lax.ppermute(value, "mpo", [(d, (d + j) % parties) for d in range(parties)])

    lanes = ring_rounds(owners) if by_ring else (0, 0)
    stages = [tuple(r for r in rounds if r <= lanes[0]) for rounds in STAGES] if by_ring else [(0,)]
    stages = [rounds for rounds in stages if rounds]
    sources = [ring_sources(owners, rounds) for rounds in stages] if by_ring else []
    shifts = np.zeros((owners, len(stages), owners), np.int32)
    stage_of = np.zeros((owners, owners), np.int32)
    for s, found in enumerate(sources):
        for d in range(owners):
            shifts[d, s] = -sectors * np.arange(owners)
            for slot, owner in enumerate(found[d]):
                shifts[d, s, owner] = sectors * (slot - owner)
                stage_of[d, owner] = s
    table = np.concatenate([shifts.reshape(owners, -1), stage_of], axis=1)
    stage_base = 1 + len(stages) * owners
    target_base = stage_base + owners
    sector_base = target_base + blocks
    left_base = sector_base + blocks
    index = jnp.concatenate(
        [
            own[None],
            jnp.asarray(table)[me],
            right_sector // sectors,
            right_sector,
            left_sector - me * sectors,
        ]
    ).astype(jnp.int32)

    def left_products(operators):
        return pl.pallas_call(
            functools.partial(
                left_kernel, parties=parties, count=len(operators), base=left_base
            ),
            out_shape=[jax.ShapeDtypeStruct((blocks, width, terms * width), jnp.bfloat16)]
            * len(operators),
            in_specs=[smem] + [anywhere] * (len(operators) + 1),
            out_specs=[vmem] * len(operators),
            scratch_shapes=[
                pltpu.VMEM((len(operators), *operators[0].shape), jnp.bfloat16),
                pltpu.VMEM(wavefunction.shape, jnp.bfloat16),
                pltpu.SemaphoreType.DMA((len(operators) + LEFT_BANDS,)),
            ],
            compiler_params=params,
            cost_estimate=pl.CostEstimate(
                flops=2 * len(operators) * blocks * terms * width**3,
                bytes_accessed=9 * 2**20,
                transcendentals=0,
            ),
            name="left_products",
        )(index, *operators, in_hbm(wavefunction))

    def right_products(lefts, pieces, spots, stage, held, slots):
        pack = width // held[2]
        return pl.pallas_call(
            functools.partial(
                right_kernel,
                lefts=len(lefts),
                spots=spots,
                parties=parties,
                stage=stage or None,
                bases=(1 + (stage or 0) * owners, stage_base, target_base, sector_base),
            ),
            out_shape=[jax.ShapeDtypeStruct((slots // pack, rows, width), jnp.bfloat16)] * parties,
            in_specs=[smem] + [vmem] * len(lefts) + [anywhere] * len(pieces),
            out_specs=[vmem] * parties,
            scratch_shapes=[
                pltpu.VMEM(held, jnp.bfloat16),
                pltpu.SMEM((slots + 1,), jnp.int32),
                pltpu.SemaphoreType.DMA((len(pieces),)),
            ],
            compiler_params=params,
            cost_estimate=pl.CostEstimate(
                flops=2 * slots * held[0] * width**2 * held[2],
                bytes_accessed=12 * 2**20,
                transcendentals=0,
            ),
            name="right_products",
        )(index, *lefts, *pieces)

    mask = term_mask.astype(left_operators.dtype)[:, :, None, None]
    masked = left_operators * mask
    if not by_ring:
        lefts = left_products([masked])
        whole = lax.all_gather(right_operators, "sec", axis=1, tiled=True)
        shape = (terms, owners * sectors, width, width)
        partial = right_products(lefts, [whole], [(0, 0)], None, shape, blocks)
        total = partial[0].astype(jnp.float32)
        for j in range(1, parties):
            total = total + to_party(partial[j], j).astype(jnp.float32)
        return total.astype(jnp.bfloat16)

    columns = width // parties
    mine = lax.dynamic_slice_in_dim(right_operators, columns * own, columns, 2)
    theirs = lax.dynamic_slice_in_dim(right_operators, columns * (1 - own), columns, 2)
    given = to_party(theirs, 1)
    other = to_party(masked, 1)
    lefts = left_products([masked, other])
    done = {"given": [given], "other": [other], "left": lefts, "masked": [masked], "index": [index]}

    def launch(name, value):
        waits = [v for w in WAITS.get(name, ()) for v in done[w]]
        done[name] = [step_round(after(value, *waits), owners)]
        return done[name][0]

    trails = []
    for n, part in enumerate((mine, given)):
        heads = [part, swap_cores(part, owners)]
        trail = {(0, 0): heads[0], (0, 1): heads[1]}
        for number in range(1, APART + 1):
            for lane in range(2):
                if number <= lanes[lane]:
                    heads[lane] = launch("PQ"[lane] + str(number) + "ox"[n], heads[lane])
                    trail[number, lane] = heads[lane]
        trails.append(trail)
    joined = {}
    kept = []
    for s, rounds in enumerate(stages):
        gathered, spots, count = [], [], 0
        for number in rounds:
            for lane in range(2):
                if number > lanes[lane] or (number == 0 and lane):
                    continue
                if number == 0:
                    found = [(n * terms, trail[0, q], q) for n, trail in enumerate(trails) for q in range(2)]
                elif number <= APART:
                    found = [
                        (n * terms, v, q)
                        for n, trail in enumerate(trails)
                        for q, v in enumerate((trail[number, lane], swap_cores(trail[number, lane], owners)))
                    ]
                else:
                    if lane not in joined:
                        joined[lane] = jnp.concatenate([trail[APART, lane] for trail in trails], axis=0)
                    head = joined[lane] = launch("PQ"[lane] + str(number), joined[lane])
                    waits = [v for w in WAITS.get("S" + str(number) + "PQ"[lane], ()) for v in done[w]]
                    found = [(0, head, 0), (0, swap_cores(after(head, *waits), owners), 1)]
                for term, piece, q in found:
                    gathered.append(piece)
                    spots.append((term, (count + q) * sectors))
                count += 2
        waits = [v for w in WAITS.get("m" + str(s), ()) for v in done[w]]
        gathered[0] = after(gathered[0], *waits)
        slots = blocks if s == 0 else min(blocks, count * sectors)
        held = (parties * terms, count * sectors, columns, width)
        partial = right_products(lefts, gathered, spots, s, held, slots)
        done["m" + str(s)] = partial
        done["y" + str(s)] = [to_party(partial[1], 1)]
        kept.append((partial[0], done["y" + str(s)][0]))

    return pl.pallas_call(
        functools.partial(join_kernel, stages=len(kept), bases=(stage_base, target_base)),
        out_shape=jax.ShapeDtypeStruct((blocks, rows, width), jnp.bfloat16),
        in_specs=[smem] + [vmem] * (2 * len(kept)),
        out_specs=anywhere,
        scratch_shapes=[
            pltpu.VMEM((blocks, rows, width), jnp.bfloat16),
            pltpu.SemaphoreType.DMA((JOIN_BANDS,)),
        ],
        compiler_params=params,
        cost_estimate=pl.CostEstimate(flops=0, bytes_accessed=4 * 2**20, transcendentals=0),
        name="join_columns",
    )(index, *[pair[0] for pair in kept], *[pair[1] for pair in kept])


def solution(mesh):
    placed = (
        P("sec", None, None),
        P("sec"),
        P("sec"),
        P("mpo", "sec"),
        P("mpo", "sec", None, None),
        P("mpo", "sec", None, None),
    )
    return jax.shard_map(
        on_device, mesh=mesh, in_specs=placed, out_specs=P("sec", "mpo", None), check_vma=False
    )
```

```python
import functools

import jax
import jax.numpy as jnp
import numpy as np
from jax import lax
from jax.experimental import pallas as pl
from jax.experimental.pallas import tpu as pltpu
from jax.sharding import PartitionSpec as P

RING_LIMIT = 16
VMEM_LIMIT = 24 * 1024 * 1024
UNROLL = 10
LEFT_BANDS = 5
JOIN_BANDS = 4
STAGES = ((0, 1, 2), (3,), (4,))
APART = 2
WAITS = {"P2o": ('masked',), "P1x": ('P2o',), "Q1x": ('Q2o',), "P2x": ('index', 'other'), "P3": ('Q2x', 'left'), "P4": ('m0',), "m1": ('y0',)}


def in_hbm(value):
    return pltpu.with_memory_space_constraint(value, pltpu.HBM)


def after(value, *others):
    return lax.optimization_barrier((value, *others))[0] if others else value


def chip_ring(chips):
    across = 2 if chips % 2 == 0 else 1
    up = [z * across for z in range(chips // across)]
    down = [z * across + 1 for z in reversed(range(chips // across))] if across == 2 else []
    return up + down


def swap_cores(value, owners):
    return lax.ppermute(value, "sec", [(d, d ^ 1) for d in range(owners)])


def step_round(value, owners):
    order = chip_ring(owners // 2)
    following = {chip: order[(i + 1) % len(order)] for i, chip in enumerate(order)}
    before = {chip: order[i - 1] for i, chip in enumerate(order)}
    pairs = [(d, 2 * (before if d % 2 else following)[d // 2] + d % 2) for d in range(owners)]
    return lax.ppermute(value, "sec", pairs)


def ring_rounds(owners):
    chips = owners // 2
    return chips // 2, (chips - 1) // 2


def ring_sources(owners, rounds):
    chips = owners // 2
    order = chip_ring(chips)
    place = {chip: i for i, chip in enumerate(order)}
    found = np.zeros((owners, 0), np.int32)
    for number in rounds:
        for lane, last in enumerate(ring_rounds(owners)):
            if number > last or (number == 0 and lane):
                continue
            for swapped in range(2):
                column = []
                for d in range(owners):
                    source = d ^ swapped
                    way = 1 if source % 2 else -1
                    chip = order[(place[d // 2] + way * number) % chips]
                    column.append(2 * chip + (source % 2) ^ lane)
                found = np.concatenate([found, np.array(column, np.int32)[:, None]], axis=1)
    return found


def left_kernel(index_ref, *refs, parties, count, base):
    operator_refs, wave_ref = refs[:count], refs[count]
    out_refs = refs[count + 1 : 2 * count + 1]
    operators, waves, arrived = refs[2 * count + 1 :]
    _, terms, _, width, _ = operators.shape
    blocks = waves.shape[0]
    rows = width // parties
    own = index_ref[0]
    copies = [
        pltpu.make_async_copy(ref, operators.at[n], arrived.at[n])
        for n, ref in enumerate(operator_refs)
    ]
    bands = blocks // LEFT_BANDS if blocks % LEFT_BANDS == 0 else blocks
    for n in range(blocks // bands):
        there = pl.ds(n * bands, bands)
        copies.append(
            pltpu.make_async_copy(wave_ref.at[there], waves.at[there], arrived.at[count + n])
        )
    for copy in copies[: count + 1]:
        copy.start()
    for copy in copies[:count]:
        copy.wait()
    for copy in copies[count + 1 :]:
        copy.start()

    def one_block(b, carry):
        local = index_ref[base + b]
        strips = [
            operators[
                n, k, local, pl.ds(pl.multiple_of(lax.rem(own + j, parties) * rows, rows), rows), :
            ]
            for n in range(count)
            for k in range(terms)
            for j in range(parties)
        ]
        product = jnp.dot(
            jnp.concatenate(strips, axis=0), waves[b], preferred_element_type=jnp.float32
        ).astype(jnp.bfloat16)
        for n, out_ref in enumerate(out_refs):
            for k in range(terms):
                start = (n * terms + k) * width
                out_ref[b, :, k * width : (k + 1) * width] = product[start : start + width]
        return carry

    for n, copy in enumerate(copies[count:]):
        copy.wait()
        lax.fori_loop(n * bands, (n + 1) * bands, one_block, 0, unroll=16)


def right_kernel(index_ref, *refs, lefts, spots, parties, stage, bases):
    pieces = len(spots)
    left_refs, piece_refs = refs[:lefts], refs[lefts : lefts + pieces]
    out_refs = refs[lefts + pieces : lefts + pieces + parties]
    held, listed, arrived = refs[lefts + pieces + parties :]
    terms, _, columns, width = held.shape
    blocks, height, _ = left_refs[0].shape
    rows, pack = height // parties, width // columns
    slots = out_refs[0].shape[0] * pack
    shift_base, stage_base, target_base, sector_base = bases

    copies = []
    for number, (piece, (term, slot)) in enumerate(zip(piece_refs, spots)):
        there = held.at[pl.ds(term, piece.shape[0]), pl.ds(slot, piece.shape[1])]
        copies.append(pltpu.make_async_copy(piece, there, arrived.at[number]))
    for copy in copies:
        copy.start()
    if stage is not None:

        def clear(i, carry):
            listed[i] = 0
            return carry

        def enlist(b, count):
            listed[count] = b
            hit = index_ref[stage_base + index_ref[target_base + b]] == stage
            return count + hit.astype(jnp.int32)

        lax.fori_loop(0, slots + 1, clear, 0, unroll=True)
        lax.fori_loop(0, blocks, enlist, jnp.int32(0), unroll=10)
    for copy in copies:
        copy.wait()
    lane = lax.broadcasted_iota(jnp.int32, (height, width), 1) // columns

    def one_group(g, carry):
        chosen = [g * pack + q for q in range(pack)]
        if stage is not None:
            chosen = [listed[i] for i in chosen]
        factors = []
        for b in chosen:
            sector = index_ref[sector_base + b] + index_ref[shift_base + index_ref[target_base + b]]
            factors.append(jnp.concatenate([held[k, sector] for k in range(terms)], axis=1))
        left = jnp.concatenate(
            [jnp.concatenate([ref[b] for b in chosen], axis=0) for ref in left_refs], axis=1
        )
        product = lax.dot_general(
            left,
            jnp.concatenate(factors, axis=0),
            (((1,), (1,)), ((), ())),
            preferred_element_type=jnp.float32,
        ).reshape(pack, height, width)
        value = product[0]
        for q in range(1, pack):
            value = jnp.where(lane == q, product[q], value)
        for j in range(parties):
            out_refs[j][g] = value[j * rows : (j + 1) * rows].astype(out_refs[j].dtype)
        return carry

    lax.fori_loop(0, slots // pack, one_group, 0, unroll=min(4 * UNROLL, slots // pack))


def join_kernel(index_ref, *refs, stages, bases):
    own_refs, other_refs = refs[:stages], refs[stages : 2 * stages]
    out_ref, joined, sent = refs[2 * stages :]
    blocks, rows, width = joined.shape
    stage_base, target_base = bases
    own = index_ref[0]
    upper = lax.broadcasted_iota(jnp.int32, (rows, width), 1) // (width // 2)

    def pick(given, places, stage):
        value = given[0][places[0]]
        for s in range(1, stages):
            value = jnp.where(stage == s, given[s][places[s]], value)
        return value.astype(jnp.float32)

    def one_block(b, counts):
        stage = index_ref[stage_base + index_ref[target_base + b]]
        slot, places, grown = b, [lax.shift_right_logical(b, 1)], []
        for s in range(1, stages):
            hit = stage == s
            slot = jnp.where(hit, counts[s - 1], slot)
            last = own_refs[s].shape[0] - 1
            places.append(jnp.minimum(lax.shift_right_logical(counts[s - 1], 1), last))
            grown.append(counts[s - 1] + hit.astype(jnp.int32))
        side = lax.bitwise_and(slot, 1)
        here = side == own
        mine, given = pick(own_refs, places, stage), pick(other_refs, places, stage)
        moved = pltpu.roll(jnp.where(here, given, mine), width // 2, 1)
        kept = jnp.where(here, mine, given)
        joined[b] = jnp.where(upper == side, kept, moved).astype(joined.dtype)
        return tuple(grown)

    counts = (jnp.int32(0),) * (stages - 1)
    bands = blocks // JOIN_BANDS if blocks % JOIN_BANDS == 0 else blocks
    copies = []
    for n in range(blocks // bands):
        counts = lax.fori_loop(n * bands, (n + 1) * bands, one_block, counts, unroll=20)
        there = pl.ds(n * bands, bands)
        copies.append(pltpu.make_async_copy(joined.at[there], out_ref.at[there], sent.at[n]))
        copies[-1].start()
    for copy in copies:
        copy.wait()


def on_device(wavefunction, left_sector, right_sector, term_mask, left_operators, right_operators):
    owners, parties = lax.axis_size("sec"), lax.axis_size("mpo")
    me, own = lax.axis_index("sec"), lax.axis_index("mpo")
    terms, sectors, width, _ = left_operators.shape
    blocks = wavefunction.shape[0]
    rows = width // parties
    smem = pl.BlockSpec(memory_space=pltpu.SMEM)
    vmem = pl.BlockSpec(memory_space=pltpu.VMEM)
    anywhere = pl.BlockSpec(memory_space=pl.ANY)
    params = pltpu.CompilerParams(vmem_limit_bytes=VMEM_LIMIT)
    by_ring = parties == 2 and owners <= RING_LIMIT and owners % 4 == 0 and blocks % 2 == 0

    def to_party(value, j):
        return lax.ppermute(value, "mpo", [(d, (d + j) % parties) for d in range(parties)])

    lanes = ring_rounds(owners) if by_ring else (0, 0)
    stages = [tuple(r for r in rounds if r <= lanes[0]) for rounds in STAGES] if by_ring else [(0,)]
    stages = [rounds for rounds in stages if rounds]
    sources = [ring_sources(owners, rounds) for rounds in stages] if by_ring else []
    shifts = np.zeros((owners, len(stages), owners), np.int32)
    stage_of = np.zeros((owners, owners), np.int32)
    for s, found in enumerate(sources):
        for d in range(owners):
            shifts[d, s] = -sectors * np.arange(owners)
            for slot, owner in enumerate(found[d]):
                shifts[d, s, owner] = sectors * (slot - owner)
                stage_of[d, owner] = s
    table = np.concatenate([shifts.reshape(owners, -1), stage_of], axis=1)
    stage_base = 1 + len(stages) * owners
    target_base = stage_base + owners
    sector_base = target_base + blocks
    left_base = sector_base + blocks
    index = jnp.concatenate(
        [
            own[None],
            jnp.asarray(table)[me],
            right_sector // sectors,
            right_sector,
            left_sector - me * sectors,
        ]
    ).astype(jnp.int32)

    def left_products(operators):
        return pl.pallas_call(
            functools.partial(
                left_kernel, parties=parties, count=len(operators), base=left_base
            ),
            out_shape=[jax.ShapeDtypeStruct((blocks, width, terms * width), jnp.bfloat16)]
            * len(operators),
            in_specs=[smem] + [anywhere] * (len(operators) + 1),
            out_specs=[vmem] * len(operators),
            scratch_shapes=[
                pltpu.VMEM((len(operators), *operators[0].shape), jnp.bfloat16),
                pltpu.VMEM(wavefunction.shape, jnp.bfloat16),
                pltpu.SemaphoreType.DMA((len(operators) + LEFT_BANDS,)),
            ],
            compiler_params=params,
            cost_estimate=pl.CostEstimate(
                flops=2 * len(operators) * blocks * terms * width**3,
                bytes_accessed=9 * 2**20,
                transcendentals=0,
            ),
            name="left_products",
        )(index, *operators, in_hbm(wavefunction))

    def right_products(lefts, pieces, spots, stage, held, slots):
        pack = width // held[2]
        return pl.pallas_call(
            functools.partial(
                right_kernel,
                lefts=len(lefts),
                spots=spots,
                parties=parties,
                stage=stage or None,
                bases=(1 + (stage or 0) * owners, stage_base, target_base, sector_base),
            ),
            out_shape=[jax.ShapeDtypeStruct((slots // pack, rows, width), jnp.bfloat16)] * parties,
            in_specs=[smem] + [vmem] * len(lefts) + [anywhere] * len(pieces),
            out_specs=[vmem] * parties,
            scratch_shapes=[
                pltpu.VMEM(held, jnp.bfloat16),
                pltpu.SMEM((slots + 1,), jnp.int32),
                pltpu.SemaphoreType.DMA((len(pieces),)),
            ],
            compiler_params=params,
            cost_estimate=pl.CostEstimate(
                flops=2 * slots * held[0] * width**2 * held[2],
                bytes_accessed=12 * 2**20,
                transcendentals=0,
            ),
            name="right_products",
        )(index, *lefts, *pieces)

    mask = term_mask.astype(left_operators.dtype)[:, :, None, None]
    masked = left_operators * mask
    if not by_ring:
        lefts = left_products([masked])
        whole = lax.all_gather(right_operators, "sec", axis=1, tiled=True)
        shape = (terms, owners * sectors, width, width)
        partial = right_products(lefts, [whole], [(0, 0)], None, shape, blocks)
        total = partial[0].astype(jnp.float32)
        for j in range(1, parties):
            total = total + to_party(partial[j], j).astype(jnp.float32)
        return total.astype(jnp.bfloat16)

    columns = width // parties
    mine = lax.dynamic_slice_in_dim(right_operators, columns * own, columns, 2)
    theirs = lax.dynamic_slice_in_dim(right_operators, columns * (1 - own), columns, 2)
    given = to_party(theirs, 1)
    other = to_party(masked, 1)
    lefts = left_products([masked, other])
    done = {"given": [given], "other": [other], "left": lefts, "masked": [masked], "index": [index]}

    def launch(name, value):
        waits = [v for w in WAITS.get(name, ()) for v in done[w]]
        done[name] = [step_round(after(value, *waits), owners)]
        return done[name][0]

    trails = []
    for n, part in enumerate((mine, given)):
        heads = [part, swap_cores(part, owners)]
        trail = {(0, 0): heads[0], (0, 1): heads[1]}
        for number in range(1, APART + 1):
            for lane in range(2):
                if number <= lanes[lane]:
                    heads[lane] = launch("PQ"[lane] + str(number) + "ox"[n], heads[lane])
                    trail[number, lane] = heads[lane]
        trails.append(trail)
    joined = {}
    kept = []
    for s, rounds in enumerate(stages):
        gathered, spots, count = [], [], 0
        for number in rounds:
            for lane in range(2):
                if number > lanes[lane] or (number == 0 and lane):
                    continue
                if number == 0:
                    found = [(n * terms, trail[0, q], q) for n, trail in enumerate(trails) for q in range(2)]
                elif number == APART and number < lanes[lane]:
                    head = joined[lane] = jnp.concatenate(
                        [trail[number, lane] for trail in trails], axis=0
                    )
                    found = [(0, head, 0), (0, swap_cores(head, owners), 1)]
                elif number <= APART:
                    found = [
                        (n * terms, v, q)
                        for n, trail in enumerate(trails)
                        for q, v in enumerate((trail[number, lane], swap_cores(trail[number, lane], owners)))
                    ]
                else:
                    if lane not in joined:
                        joined[lane] = jnp.concatenate([trail[APART, lane] for trail in trails], axis=0)
                    head = joined[lane] = launch("PQ"[lane] + str(number), joined[lane])
                    waits = [v for w in WAITS.get("S" + str(number) + "PQ"[lane], ()) for v in done[w]]
                    found = [(0, head, 0), (0, swap_cores(after(head, *waits), owners), 1)]
                for term, piece, q in found:
                    gathered.append(piece)
                    spots.append((term, (count + q) * sectors))
                count += 2
        waits = [v for w in WAITS.get("m" + str(s), ()) for v in done[w]]
        gathered[0] = after(gathered[0], *waits)
        slots = blocks if s == 0 else min(blocks, count * sectors)
        held = (parties * terms, count * sectors, columns, width)
        partial = right_products(lefts, gathered, spots, s, held, slots)
        done["m" + str(s)] = partial
        done["y" + str(s)] = [to_party(partial[1], 1)]
        kept.append((partial[0], done["y" + str(s)][0]))

    return pl.pallas_call(
        functools.partial(join_kernel, stages=len(kept), bases=(stage_base, target_base)),
        out_shape=jax.ShapeDtypeStruct((blocks, rows, width), jnp.bfloat16),
        in_specs=[smem] + [vmem] * (2 * len(kept)),
        out_specs=anywhere,
        scratch_shapes=[
            pltpu.VMEM((blocks, rows, width), jnp.bfloat16),
            pltpu.SemaphoreType.DMA((JOIN_BANDS,)),
        ],
        compiler_params=params,
        cost_estimate=pl.CostEstimate(flops=0, bytes_accessed=4 * 2**20, transcendentals=0),
        name="join_columns",
    )(index, *[pair[0] for pair in kept], *[pair[1] for pair in kept])


def solution(mesh):
    placed = (
        P("sec", None, None),
        P("sec"),
        P("sec"),
        P("mpo", "sec"),
        P("mpo", "sec", None, None),
        P("mpo", "sec", None, None),
    )
    return jax.shard_map(
        on_device, mesh=mesh, in_specs=placed, out_specs=P("sec", "mpo", None), check_vma=False
    )
```
